32 devices in a mesh: pipe: 8 (over z, core), tensor: 4 (over y, x).
Axes of the slice: x: 2, y: 2, z: 4, core: 2. Of those that a mesh axis runs over, the one named last changes fastest.
Arguments:
- section_inputs: bfloat16 [8, 8, 128, 12288], P('pipe', None, None, 'tensor'), may hold values from -6 to 6
- out_grad: bfloat16 [8, 128, 12288], P(None, None, 'tensor'), may hold values from -6 to 6
- w_first: bfloat16 [8, 1, 96, 128, 128], P('pipe', None, 'tensor'), may hold values from -0.5 to 0.5
- w_second: bfloat16 [8, 1, 96, 128, 128], P('pipe', None, 'tensor'), may hold values from -0.5 to 0.5
- drop_flags: int32 [8, 1], P('pipe'), may hold values 0 or 1
- perm: int32 [8, 1, 12288], P('pipe'), may hold values from 0 to 12287, as said below
Outputs:
- input_grads: bfloat16 [8, 8, 128, 12288], P('pipe', None, None, 'tensor')
- grad_first: float32 [8, 1, 96, 128, 128], P('pipe', None, 'tensor')
- grad_second: float32 [8, 1, 96, 128, 128], P('pipe', None, 'tensor')
The draws below stay inside these ranges and needn't reach their ends.
Inputs may be any that keep to these rules, and one draw needn't show every extreme that they name: For each section and layer, perm is a permutation of 0 to 12287, and for every two block groups g and h exactly 768 of the positions h * 3072 to (h + 1) * 3072 - 1 hold a feature of group g, that is a number from g * 3072 to (g + 1) * 3072 - 1.
All inputs are finite; a program needn't handle non-finite values. No bound on the sum of `drop_flags` on one device may be relied on, other than what follows from the above.
Results may differ from the reference program's by a relative error of at most 0.023.
Values may be sent and summed in bfloat16 or wider, within the bound.
A program may use at most 128 MiB of HBM per device.

```python
import jax
import jax.numpy as jnp

NB = 96
BS = 128
W = 12288
TOK = 128
MB = 8
LAYERS = 1
SECTIONS = 8
GROUPS = 4


def draw_perm(key, part):
    feat_count = W // GROUPS
    per_peer = feat_count // GROUPS

    def one_layer(layer_key):
        first_key, second_key = jax.random.split(layer_key)
        spread = jax.vmap(lambda k: jax.random.permutation(k, feat_count))(jax.random.split(first_key, GROUPS))
        starts = jnp.arange(GROUPS, dtype=jnp.int32)[:, None] * feat_count
        sources = (starts + spread.astype(jnp.int32)).reshape(GROUPS, GROUPS, per_peer)
        arrived = jnp.transpose(sources, (1, 0, 2)).reshape(GROUPS, feat_count)
        placed = jax.vmap(lambda k: jax.random.permutation(k, feat_count))(jax.random.split(second_key, GROUPS))
        inverse_place = jnp.argsort(placed, axis=1)
        return jnp.take_along_axis(arrived, inverse_place, axis=1).reshape(W)
    keys = jax.random.split(key, SECTIONS * LAYERS)
    return jax.vmap(one_layer)(keys).reshape(SECTIONS, LAYERS, W).astype(jnp.int32)


def set_ends(entries, own_key, least, largest):
    index_at = [jax.random.randint(jax.random.fold_in(own_key, axis), (), 0, length) for axis, length in enumerate(entries.shape)]
    longest = entries.shape.index(max(entries.shape))
    beside = index_at[:longest] + [(index_at[longest] + 1) % entries.shape[longest]] + index_at[longest + 1:]
    return entries.at[tuple(index_at)].set(least).at[tuple(beside)].set(largest)


def steps_of(key, extent, cuts, least, high):
    level, own = 1.0, jax.random.fold_in(key, 6)
    for position, blocks in cuts:
        heights = jnp.exp(jax.random.uniform(jax.random.fold_in(own, position), (blocks,), jnp.float32, least / len(cuts), high / len(cuts)))
        level = level * jnp.repeat(heights, extent[position] // blocks).reshape([-1 if axis == position else 1 for axis in range(len(extent))])
    return level


def centred(rng, extent, deviation, most, pieces=(), kind=jnp.bfloat16):
    loudness = steps_of(rng, extent, pieces, -0.22, 0.18) if pieces else 1.0
    entries = jax.random.normal(rng, extent, jnp.float32) * deviation * loudness
    return jnp.minimum(jnp.maximum(entries, -most), most).astype(kind)


def setup_inputs(seed: int = 0) -> dict:
    arg_keys = jax.random.split(jax.random.key(seed), 7)
    return {
        "section_inputs": centred(arg_keys[0], (SECTIONS, MB, TOK, W), 1.0, 6.0, ((0, 8), (3, 4))),
        "out_grad": centred(arg_keys[1], (MB, TOK, W), 1.0, 6.0, ((2, 4),)),
        "w_first": centred(arg_keys[2], (SECTIONS, LAYERS, NB, BS, BS), BS ** -0.5, 0.5, ((0, 8), (2, 4))),
        "w_second": centred(arg_keys[3], (SECTIONS, LAYERS, NB, BS, BS), BS ** -0.5, 0.5, ((0, 8), (2, 4))),
        "drop_flags": set_ends((jax.random.randint(arg_keys[4], (SECTIONS, LAYERS), 0, 4) < 3).astype(jnp.int32), jax.random.fold_in(arg_keys[4], 1), 0, 1),
        "perm": draw_perm(jax.random.fold_in(arg_keys[6], 71), 0),
    }


gelu_scale = 0.7978845608028654
gelu_cubic = 0.044715


def gelu_value(values):
    inner = gelu_scale * (values + gelu_cubic * values * values * values)
    return 0.5 * values * (1.0 + jnp.tanh(inner))


def gelu_slope(values):
    tangent = jnp.tanh(gelu_scale * (values + gelu_cubic * values * values * values))
    return 0.5 * (1.0 + tangent) + 0.5 * values * (1.0 - tangent * tangent) * gelu_scale * (1.0 + 3.0 * gelu_cubic * values * values)


def blocked(values):
    return values.reshape(values.shape[:-1] + (NB, BS)).astype(jnp.float32)


def block_product(values, weight):
    result = jnp.einsum('mtbi,bij->mtbj', blocked(values), weight.astype(jnp.float32))
    return result.reshape(values.shape)


def block_back(values, weight):
    result = jnp.einsum('mtbj,bij->mtbi', blocked(values), weight.astype(jnp.float32))
    return result.reshape(values.shape)


def block_outer(left, right):
    return jnp.einsum('mtbi,mtbj->bij', blocked(left), blocked(right))


def reference(section_inputs, out_grad, w_first, w_second, drop_flags, perm):
    cotangent = out_grad
    grads_in = []
    grads_first = []
    grads_second = []
    for section_index in range(SECTIONS - 1, -1, -1):
        layer_inputs = [section_inputs[section_index]]
        saved_pairs = []
        for layer_index in range(LAYERS):
            current = layer_inputs[-1]
            keep_factor = drop_flags[section_index, layer_index].astype(jnp.float32)
            before = block_product(current, w_first[section_index, layer_index])
            hidden = gelu_value(before).astype(jnp.bfloat16)
            mixed = jnp.take(hidden, perm[section_index, layer_index], axis=2)
            branch = block_product(mixed, w_second[section_index, layer_index])
            layer_inputs.append((current.astype(jnp.float32) + keep_factor * branch).astype(jnp.bfloat16))
            saved_pairs.append((before, mixed))
        grad_now = cotangent
        first_list = []
        second_list = []
        for layer_index in range(LAYERS - 1, -1, -1):
            current = layer_inputs[layer_index]
            before, mixed = saved_pairs[layer_index]
            keep_factor = drop_flags[section_index, layer_index].astype(jnp.float32)
            grad_branch = (keep_factor * grad_now.astype(jnp.float32)).astype(jnp.bfloat16)
            second_list.append(block_outer(mixed, grad_branch))
            grad_mixed = block_back(grad_branch, w_second[section_index, layer_index]).astype(jnp.bfloat16)
            inverse = jnp.argsort(perm[section_index, layer_index]).astype(jnp.int32)
            grad_hidden = jnp.take(grad_mixed, inverse, axis=2)
            grad_before = (grad_hidden.astype(jnp.float32) * gelu_slope(before)).astype(jnp.bfloat16)
            first_list.append(block_outer(current, grad_before))
            grad_now = (grad_now.astype(jnp.float32) + block_back(grad_before, w_first[section_index, layer_index])).astype(jnp.bfloat16)
        cotangent = grad_now
        grads_in.append(grad_now)
        grads_first.append(jnp.stack(first_list[::-1]))
        grads_second.append(jnp.stack(second_list[::-1]))
    return (jnp.stack(grads_in[::-1]), jnp.stack(grads_first[::-1]), jnp.stack(grads_second[::-1]))
```

```python
import jax
import jax.numpy as jnp
from jax import lax
from jax.sharding import PartitionSpec as P

gelu_scale = 0.7978845608028654
gelu_cubic = 0.044715
LANES = 128


def gelu_both(values):
    square = values * values
    tangent = jnp.tanh(gelu_scale * (values + gelu_cubic * square * values))
    value = 0.5 * values * (1.0 + tangent)
    slope = 0.5 * (1.0 + tangent) + 0.5 * values * (1.0 - tangent * tangent) * gelu_scale * (
        1.0 + 3.0 * gelu_cubic * square
    )
    return value, slope


def block_product(values, weight, spec):
    count, size, _ = weight.shape
    split = values.reshape(values.shape[0], count, size)
    result = jnp.einsum(spec, split, weight, preferred_element_type=jnp.float32)
    return result.reshape(values.shape)


def block_outer(left, right, count):
    left_blocks = left.reshape(left.shape[0], count, -1)
    right_blocks = right.reshape(right.shape[0], count, -1)
    return jnp.einsum("tbi,tbj->bij", left_blocks, right_blocks, preferred_element_type=jnp.float32)


def running_rank(member):
    rows, width = member.shape
    tile = LANES
    pieces = member.reshape(rows, width // tile, tile).astype(jnp.bfloat16)
    upper = jnp.triu(jnp.ones((tile, tile), jnp.bfloat16))
    inner = jnp.einsum("rbi,ij->rbj", pieces, upper, preferred_element_type=jnp.float32)
    totals = inner[:, :, -1].astype(jnp.bfloat16)
    blocks = width // tile
    strict = jnp.triu(jnp.ones((blocks, blocks), jnp.bfloat16), 1)
    before = jnp.einsum("rb,bc->rc", totals, strict, preferred_element_type=jnp.float32)
    return (inner + before[:, :, None]).reshape(rows, width).astype(jnp.int32) - 1


def mixing(source_row, group_index, group_count):
    feat_count = source_row.shape[0] // group_count
    per_peer = feat_count // group_count
    slots = -(-per_peer // LANES) * LANES
    targets = source_row.reshape(group_count, feat_count)
    groups = targets // feat_count
    place = jnp.arange(slots, dtype=jnp.int32)

    mine = groups == group_index
    rank = jnp.where(mine, running_rank(mine), -1)
    feature = targets - group_index * feat_count
    hit = rank[:, None, :] == place[None, :, None]
    chosen = jnp.sum(jnp.where(hit, feature[:, None, :] + 1, 0), axis=2) - 1
    leaving = (chosen[:, :, None] == jnp.arange(feat_count, dtype=jnp.int32)).astype(jnp.bfloat16)

    own = lax.dynamic_index_in_dim(groups, group_index, 0, keepdims=False)
    member = own[None, :] == jnp.arange(group_count, dtype=jnp.int32)[:, None]
    own_rank = jnp.where(member, running_rank(member), -1)
    landing = (own_rank[:, None, :] == place[None, :, None]).astype(jnp.bfloat16)
    return leaving, landing


def exchange(values):
    return lax.all_to_all(values, "tensor", split_axis=0, concat_axis=0, tiled=True)


def relay(cotangents, slopes, back_mix, leaving, first_weights):
    section_count = lax.axis_size("pipe")
    section_index = lax.axis_index("pipe")
    micro_count = cotangents.shape[0]
    route = [(i, i - 1) for i in range(1, section_count)]

    def advance(step, carry):
        outgoing, grads, befores = carry
        incoming = lax.ppermute(outgoing, "pipe", route)
        micro = step - (section_count - 1 - section_index)
        live = (micro >= 0) & (micro < micro_count)
        micro = jnp.clip(micro, 0, micro_count - 1)
        last = lax.dynamic_index_in_dim(cotangents, micro, 0, keepdims=False)
        grad_now = jnp.where(section_index == section_count - 1, last, incoming)
        sent = jnp.einsum(
            "tj,hjk->htk", grad_now, back_mix, preferred_element_type=jnp.float32
        ).astype(jnp.bfloat16)
        came = exchange(sent)
        hidden = jnp.einsum("htk,hkf->tf", came, leaving, preferred_element_type=jnp.float32)
        slope = lax.dynamic_index_in_dim(slopes, micro, 0, keepdims=False)
        before = (hidden * slope.astype(jnp.float32)).astype(jnp.bfloat16)
        back = block_product(before, first_weights, "tbj,bij->tbi")
        grad = (grad_now.astype(jnp.float32) + back).astype(jnp.bfloat16)

        def keep(buffer, value):
            old = lax.dynamic_index_in_dim(buffer, micro, 0, keepdims=False)
            return lax.dynamic_update_index_in_dim(buffer, jnp.where(live, value, old), micro, 0)

        return grad, keep(grads, grad), keep(befores, before)

    empty = jnp.zeros(cotangents.shape, jnp.bfloat16)
    start = (jnp.zeros(cotangents.shape[1:], jnp.bfloat16), empty, empty)
    _, grads, befores = lax.fori_loop(0, micro_count + section_count - 1, advance, start)
    return grads, befores


def on_device(section_inputs, out_grad, w_first, w_second, drop_flags, perm):
    section_count = lax.axis_size("pipe")
    section_index = lax.axis_index("pipe")
    group_count = lax.axis_size("tensor")
    group_index = lax.axis_index("tensor")
    _, micro_count, token_count, feat_count = section_inputs.shape
    first_weights = w_first[0, 0]
    second_weights = w_second[0, 0]
    block_count, size, _ = first_weights.shape
    kept = drop_flags[0, 0].astype(jnp.bfloat16)
    leaving, landing = mixing(perm[0, 0], group_index, group_count)
    slots = leaving.shape[1]

    inputs = section_inputs[0].reshape(-1, feat_count)
    before = block_product(inputs, first_weights, "tbi,bij->tbj")
    hidden, slopes = gelu_both(before)
    sent = jnp.einsum(
        "tf,hkf->htk", hidden.astype(jnp.bfloat16), leaving, preferred_element_type=jnp.float32
    ).astype(jnp.bfloat16)
    came = exchange(sent)
    mixed = jnp.einsum(
        "qtk,qkp->tp", came, landing, preferred_element_type=jnp.float32
    ).astype(jnp.bfloat16)

    back_mix = jnp.einsum(
        "bij,qkbi->qbjk",
        second_weights * kept,
        landing.reshape(group_count, slots, block_count, size),
        preferred_element_type=jnp.float32,
    ).astype(jnp.bfloat16).reshape(group_count, feat_count, slots)

    chunked = (micro_count, token_count, feat_count)
    grads, befores = relay(
        out_grad, slopes.astype(jnp.bfloat16).reshape(chunked), back_mix, leaving, first_weights
    )
    arrived = lax.ppermute(grads, "pipe", [(i, i - 1) for i in range(1, section_count)])
    cotangent = jnp.where(section_index == section_count - 1, out_grad, arrived)
    branch = cotangent.reshape(-1, feat_count) * kept
    second_grad = block_outer(mixed, branch, block_count)
    first_grad = block_outer(inputs, befores.reshape(-1, feat_count), block_count)
    return grads[None], first_grad[None, None], second_grad[None, None]


def solution(mesh):
    placed = (
        P("pipe", None, None, "tensor"),
        P(None, None, "tensor"),
        P("pipe", None, "tensor", None, None),
        P("pipe", None, "tensor", None, None),
        P("pipe", None),
        P("pipe", None, None),
    )
    return jax.shard_map(
        on_device,
        mesh=mesh,
        in_specs=placed,
        out_specs=(
            P("pipe", None, None, "tensor"),
            P("pipe", None, "tensor", None, None),
            P("pipe", None, "tensor", None, None),
        ),
        check_vma=False,
    )
```

```python
import functools

import jax
import jax.numpy as jnp
from jax import lax
from jax.experimental import pallas as pl
from jax.experimental.pallas import tpu as pltpu
from jax.sharding import PartitionSpec as P

gelu_scale = 0.7978845608028654
gelu_cubic = 0.044715
LANES = 128
ROWS = 64
MESH = pl.DeviceIdType.MESH


def gelu_both(values):
    square = values * values
    tangent = jnp.tanh(gelu_scale * (values + gelu_cubic * square * values))
    value = 0.5 * values * (1.0 + tangent)
    slope = 0.5 * (1.0 + tangent) + 0.5 * values * (1.0 - tangent * tangent) * gelu_scale * (
        1.0 + 3.0 * gelu_cubic * square
    )
    return value, slope


def running_rank(member):
    rows, width = member.shape
    tile = LANES
    pieces = member.reshape(rows, width // tile, tile).astype(jnp.bfloat16)
    upper = jnp.triu(jnp.ones((tile, tile), jnp.bfloat16))
    inner = jnp.einsum("rbi,ij->rbj", pieces, upper, preferred_element_type=jnp.float32)
    totals = inner[:, :, -1].astype(jnp.bfloat16)
    blocks = width // tile
    strict = jnp.triu(jnp.ones((blocks, blocks), jnp.bfloat16), 1)
    before = jnp.einsum("rb,bc->rc", totals, strict, preferred_element_type=jnp.float32)
    return (inner + before[:, :, None]).reshape(rows, width).astype(jnp.int32) - 1


def mixing(source_row, group_index, group_count):
    feat_count = source_row.shape[0] // group_count
    per_peer = feat_count // group_count
    slots = -(-per_peer // LANES) * LANES
    targets = source_row.reshape(group_count, feat_count)
    groups = targets // feat_count
    place = jnp.arange(slots, dtype=jnp.int32)

    mine = groups == group_index
    rank = jnp.where(mine, running_rank(mine), -1)
    feature = targets - group_index * feat_count
    hit = rank[:, None, :] == place[None, :, None]
    chosen = jnp.sum(jnp.where(hit, feature[:, None, :] + 1, 0), axis=2) - 1

    own = lax.dynamic_index_in_dim(groups, group_index, 0, keepdims=False)
    sources = jnp.arange(group_count, dtype=jnp.int32)[:, None]
    member = own[None, :] == sources
    landing = jnp.sum(jnp.where(member, running_rank(member) + sources * slots, 0), axis=0)
    return chosen.reshape(-1), landing, slots


def dot(left, right, left_dim=1, right_dim=0):
    return lax.dot_general(
        left, right, (((left_dim,), (right_dim,)), ((), ())), preferred_element_type=jnp.float32
    )


def relay_kernel(
    sections, groups, slots,
    inputs, last_grads, first, first_turned, second_turned, chosen, landing,
    grads_out, befores_out, cotangents_out, came_out, sent_out, slopes_out,
    leaving, back_mix, cotangents, arrived, slopes, grads, befores, sending,
    in_sem, slope_sem, grad_sem, before_sem, sent_sem, keep_sem,
    send_sem, recv_sem, relay_send, relay_recv, swap_send, swap_recv, swap_own,
):
    section = lax.axis_index("pipe")
    group = lax.axis_index("tensor")
    last = sections - 1
    chunks, rows, feats = inputs.shape
    size = first.shape[1]
    depth = arrived.shape[0]
    tile = 512 if feats % 512 == 0 else 256

    def peer(offset):
        return lax.rem(group + offset, groups)

    def source(offset):
        return lax.rem(group + (groups - offset), groups)

    barrier = pltpu.get_barrier_semaphore()
    for offset in range(1, groups):
        pl.semaphore_signal(barrier, inc=1, device_id={"tensor": peer(offset)}, device_id_type=MESH)

    for beside in (lax.rem(section + 1, sections), lax.rem(section + last, sections)):
        pl.semaphore_signal(barrier, inc=1, device_id={"pipe": beside}, device_id_type=MESH)
    pl.semaphore_wait(barrier, groups + 1)

    def load_last(chunk):
        return pltpu.make_async_copy(
            last_grads.at[chunk], cotangents.at[chunk], relay_recv.at[chunk]
        )

    @pl.when(section == last)
    def _():
        lax.fori_loop(0, chunks, lambda m, _: (load_last(m).start(), 0)[1], 0)

    def load_input(chunk, slot):
        return pltpu.make_async_copy(inputs.at[chunk], grads.at[slot], in_sem.at[slot])

    load_input(0, 0).start()

    step = 256

    def build_leaving(index, _):
        at = pl.ds(pl.multiple_of(index * LANES, LANES), LANES)
        column = chosen[at, :]
        for left in range(0, feats, step):
            lane = lax.broadcasted_iota(jnp.int32, (LANES, step), 1) + left
            leaving[at, left : left + step] = jnp.where(column == lane, 1.0, 0.0).astype(jnp.bfloat16)
        return 0

    lax.fori_loop(0, groups * slots // LANES, build_leaving, 0)

    def build_back(block, _):
        at = pl.ds(pl.multiple_of(block * size, size), size)
        column = landing[at, :]
        turned = second_turned[block]
        for peer_index in range(groups):
            for left in range(0, slots, LANES):
                lane = lax.broadcasted_iota(jnp.int32, (size, LANES), 1) + (peer_index * slots + left)
                spread = jnp.where(column == lane, 1.0, 0.0).astype(jnp.bfloat16)
                back_mix[peer_index, at, left : left + LANES] = dot(turned, spread).astype(jnp.bfloat16)
        return 0

    lax.fori_loop(0, feats // size, build_back, 0)

    def store_slope(chunk, slot):
        return pltpu.make_async_copy(befores.at[slot], slopes_out.at[chunk], before_sem.at[slot])

    def store_sent(chunk, slot):
        return pltpu.make_async_copy(sending.at[slot], sent_out.at[:, chunk], sent_sem.at[slot])

    def forward(chunk, _):
        slot = lax.rem(chunk, 2)
        load_input(chunk, slot).wait()

        @pl.when(chunk + 1 < chunks)
        def _():
            load_input(chunk + 1, 1 - slot).start()

        @pl.when(chunk >= 2)
        def _():
            store_slope(chunk - 2, slot).wait()
            store_sent(chunk - 2, slot).wait()

        def one_block(block, _):
            at = pl.ds(pl.multiple_of(block * size, size), size)
            value, slope = gelu_both(dot(grads[slot, :, at], first[block]))
            slopes[0, :, at] = value.astype(jnp.bfloat16)
            befores[slot, :, at] = slope.astype(jnp.bfloat16)
            return 0

        lax.fori_loop(0, feats // size, one_block, 0, unroll=2)
        for target in range(groups):
            sending[slot, target] = dot(
                slopes[0], leaving[target * slots : (target + 1) * slots, :], 1, 1
            ).astype(jnp.bfloat16)
        store_slope(chunk, slot).start()
        store_sent(chunk, slot).start()
        return 0

    lax.fori_loop(0, chunks, forward, 0)
    for chunk in range(chunks - 2, chunks):
        store_slope(chunk, chunk % 2).wait()
        store_sent(chunk, chunk % 2).wait()

    def swap(offset):
        return pltpu.make_async_remote_copy(
            src_ref=sent_out.at[peer(offset)],
            dst_ref=came_out.at[group],
            send_sem=swap_send.at[offset],
            recv_sem=swap_recv.at[offset],
            device_id={"tensor": peer(offset)},
            device_id_type=MESH,
        )

    own_swap = pltpu.make_async_copy(sent_out.at[group], came_out.at[group], swap_own)

    def start_swap():
        for offset in range(1, groups):
            swap(offset).start()
        own_swap.start()

    @pl.when(section * 2 < sections)
    def _():
        start_swap()

    def mix_copy(chunk, slot, offset):
        target = peer(offset)
        return pltpu.make_async_remote_copy(
            src_ref=sending.at[slot, target],
            dst_ref=arrived.at[lax.rem(chunk, depth), group],
            send_sem=send_sem.at[slot, offset],
            recv_sem=recv_sem.at[chunk, offset],
            device_id={"tensor": target},
            device_id_type=MESH,
        )

    def mix_wait(chunk, slot, offset):
        origin = source(offset)
        pltpu.make_async_remote_copy(
            src_ref=sending.at[slot, origin],
            dst_ref=arrived.at[lax.rem(chunk, depth), origin],
            send_sem=send_sem.at[slot, offset],
            recv_sem=recv_sem.at[chunk, offset],
            device_id={"tensor": origin},
            device_id_type=MESH,
        ).wait_recv()

    def relay_copy(chunk, slot, target):
        return pltpu.make_async_remote_copy(
            src_ref=grads.at[slot],
            dst_ref=cotangents.at[chunk],
            send_sem=relay_send.at[slot],
            recv_sem=relay_recv.at[chunk],
            device_id={"pipe": target},
            device_id_type=MESH,
        )

    def load_slope(chunk, slot):
        return pltpu.make_async_copy(slopes_out.at[chunk], slopes.at[slot], slope_sem.at[slot])

    def store_cotangent(chunk):
        return pltpu.make_async_copy(
            cotangents.at[chunk], cotangents_out.at[chunk], keep_sem.at[chunk]
        )

    def store_grad(chunk, slot):
        return pltpu.make_async_copy(grads.at[slot], grads_out.at[chunk], grad_sem.at[slot])

    def store_before(chunk, slot):
        return pltpu.make_async_copy(befores.at[slot], befores_out.at[chunk], before_sem.at[slot])

    def first_half(chunk, slot):
        @pl.when(section == last)
        def _():
            load_last(chunk).wait()

        @pl.when(section < last)
        def _():
            relay_copy(chunk, slot, section + 1).wait_recv()

        load_slope(chunk, slot).start()
        store_cotangent(chunk).start()
        for offset in range(1, groups):
            target = peer(offset)
            sending[slot, target] = dot(cotangents[chunk], back_mix[target]).astype(jnp.bfloat16)
            mix_copy(chunk, slot, offset).start()
        arrived[lax.rem(chunk, depth), group] = dot(cotangents[chunk], back_mix[group]).astype(
            jnp.bfloat16
        )

    def leave(chunk, slot):
        store_grad(chunk, slot).wait()
        store_before(chunk, slot).wait()

        @pl.when(section > 0)
        def _():
            relay_copy(chunk, slot, section - 1).wait_send()

    def second_half(chunk, slot):
        for offset in range(1, groups):
            mix_wait(chunk, slot, offset)
        load_slope(chunk, slot).wait()

        @pl.when(chunk >= 2)
        def _():
            leave(chunk - 2, slot)

        held = lax.rem(chunk, depth)

        def one_tile(index, _):
            start = pl.multiple_of(index * tile, tile)
            at = pl.ds(start, tile)
            total = dot(arrived[held, 0], leaving[0:slots, at])
            for origin in range(1, groups):
                total += dot(
                    arrived[held, origin], leaving[origin * slots : (origin + 1) * slots, at]
                )
            before = (total * slopes[slot, :, at].astype(jnp.float32)).astype(jnp.bfloat16)
            befores[slot, :, at] = before
            for piece in range(tile // size):
                here = pl.ds(pl.multiple_of(start + piece * size, size), size)
                back = dot(
                    before[:, piece * size : (piece + 1) * size],
                    first_turned[index * (tile // size) + piece],
                )
                grads[slot, :, here] = (
                    cotangents[chunk, :, here].astype(jnp.float32) + back
                ).astype(jnp.bfloat16)
            return 0

        lax.fori_loop(0, feats // tile, one_tile, 0)

        @pl.when(section > 0)
        def _():
            relay_copy(chunk, slot, section - 1).start()

        store_grad(chunk, slot).start()
        store_before(chunk, slot).start()
        for offset in range(1, groups):
            mix_copy(chunk, slot, offset).wait_send()

    first_half(0, 0)

    def advance(chunk, _):
        slot = lax.rem(chunk, 2)

        @pl.when(chunk + 1 < chunks)
        def _():
            first_half(chunk + 1, 1 - slot)

        second_half(chunk, slot)
        return 0

    lax.fori_loop(0, chunks, advance, 0)

    @pl.when(section * 2 >= sections)
    def _():
        start_swap()

    for chunk in range(chunks - 2, chunks):
        leave(chunk, chunk % 2)
    lax.fori_loop(0, chunks, lambda m, _: (store_cotangent(m).wait(), 0)[1], 0)
    for offset in range(1, groups):
        swap(offset).wait()
    own_swap.wait()


def weight_kernel(came, landing, kept, cotangents, inputs, befores, first_out, second_out):
    groups, tokens, slots = came.shape
    count, size, _ = first_out.shape
    where = landing[...]
    mixed = jnp.zeros((tokens, where.shape[1]), jnp.float32)
    for origin in range(groups):
        slot = lax.broadcasted_iota(jnp.int32, (slots, where.shape[1]), 0) + origin * slots
        spread = jnp.where(slot == where, 1.0, 0.0).astype(jnp.bfloat16)
        mixed += dot(came[origin], spread)
    mixed = mixed.astype(jnp.bfloat16)
    for piece in range(count):
        at = slice(piece * size, (piece + 1) * size)
        second_out[piece] = dot(mixed[:, at], cotangents[:, at], 0, 0) * kept[0, 0]
        first_out[piece] = dot(inputs[:, at], befores[:, at], 0, 0)


def on_device(section_inputs, out_grad, w_first, w_second, drop_flags, perm):
    sections = lax.axis_size("pipe")
    groups = lax.axis_size("tensor")
    _, micro_count, token_count, feats = section_inputs.shape
    tokens = micro_count * token_count
    first = w_first[0, 0]
    blocks, size, _ = first.shape
    kept = drop_flags[0, 0]
    chosen, landing, slots = mixing(perm[0, 0], lax.axis_index("tensor"), groups)
    rows = ROWS
    chunks = tokens // rows
    depth = min(4, chunks)
    chunked = (chunks, rows, feats)

    def made(*shape):
        return jax.ShapeDtypeStruct(shape, jnp.bfloat16)

    def room(*shape):
        return pltpu.VMEM(shape, jnp.bfloat16)

    sem = pltpu.SemaphoreType.DMA
    anywhere = pl.BlockSpec(memory_space=pl.ANY)
    vmem = pl.BlockSpec(memory_space=pltpu.VMEM)
    swapped = (groups, chunks, rows, slots)
    grads, befores, cotangents, came, _, _ = pl.pallas_call(
        functools.partial(relay_kernel, sections, groups, slots),
        out_shape=[made(*chunked)] * 3 + [made(*swapped)] * 2 + [made(*chunked)],
        in_specs=[anywhere] * 2 + [vmem] * 5,
        out_specs=[anywhere] * 6,
        scratch_shapes=[
            room(groups * slots, feats),
            room(groups, feats, slots),
            room(*chunked),
            room(depth, groups, rows, slots),
            room(2, rows, feats),
            room(2, rows, feats),
            room(2, rows, feats),
            room(2, groups, rows, slots),
            sem((2,)), sem((2,)), sem((2,)), sem((2,)), sem((2,)), sem((chunks,)),
            sem((2, groups)), sem((chunks, groups)), sem((2,)), sem((chunks,)),
            sem((groups,)), sem((groups,)), sem(()),
        ],
        compiler_params=pltpu.CompilerParams(
            collective_id=0, has_side_effects=True, vmem_limit_bytes=62 * 2**20
        ),
    )(
        section_inputs.reshape(chunked),
        out_grad.reshape(chunked),
        first,
        jnp.swapaxes(first, 1, 2),
        jnp.swapaxes(w_second[0, 0], 1, 2) * kept.astype(jnp.bfloat16),
        chosen[:, None],
        landing[:, None],
    )

    wide = 256
    tall = pl.BlockSpec((tokens, wide), lambda i: (0, i))
    out = pl.BlockSpec((wide // size, size, size), lambda i: (i, 0, 0))
    weights = jax.ShapeDtypeStruct((blocks, size, size), jnp.float32)
    first_grad, second_grad = pl.pallas_call(
        weight_kernel,
        grid=(feats // wide,),
        out_shape=[weights] * 2,
        in_specs=[
            pl.BlockSpec((groups, tokens, slots), lambda i: (0, 0, 0)),
            pl.BlockSpec((1, wide), lambda i: (0, i)),
            pl.BlockSpec(memory_space=pltpu.SMEM),
            tall, tall, tall,
        ],
        out_specs=[out] * 2,
        compiler_params=pltpu.CompilerParams(vmem_limit_bytes=56 * 2**20),
    )(
        came.reshape(groups, tokens, slots),
        landing[None, :],
        kept.astype(jnp.float32).reshape(1, 1),
        cotangents.reshape(tokens, feats),
        section_inputs.reshape(tokens, feats),
        befores.reshape(tokens, feats),
    )
    return grads.reshape(section_inputs.shape), first_grad[None, None], second_grad[None, None]


def solution(mesh):
    placed = (
        P("pipe", None, None, "tensor"),
        P(None, None, "tensor"),
        P("pipe", None, "tensor", None, None),
        P("pipe", None, "tensor", None, None),
        P("pipe", None),
        P("pipe", None, None),
    )
    return jax.shard_map(
        on_device,
        mesh=mesh,
        in_specs=placed,
        out_specs=(
            P("pipe", None, None, "tensor"),
            P("pipe", None, "tensor", None, None),
            P("pipe", None, "tensor", None, None),
        ),
        check_vma=False,
    )
```

```python
import functools

import jax
import jax.numpy as jnp
from jax import lax
from jax.experimental import pallas as pl
from jax.experimental.pallas import tpu as pltpu
from jax.sharding import PartitionSpec as P

gelu_scale = 0.7978845608028654
gelu_cubic = 0.044715
LANES = 128
ROWS = 128
MESH = pl.DeviceIdType.MESH


def gelu_both(values):
    square = values * values
    tangent = jnp.tanh(gelu_scale * (values + gelu_cubic * square * values))
    value = 0.5 * values * (1.0 + tangent)
    slope = 0.5 * (1.0 + tangent) + 0.5 * values * (1.0 - tangent * tangent) * gelu_scale * (
        1.0 + 3.0 * gelu_cubic * square
    )
    return value, slope


def running_rank(member):
    rows, width = member.shape
    tile = LANES
    pieces = member.reshape(rows, width // tile, tile).astype(jnp.bfloat16)
    upper = jnp.triu(jnp.ones((tile, tile), jnp.bfloat16))
    inner = jnp.einsum("rbi,ij->rbj", pieces, upper, preferred_element_type=jnp.float32)
    totals = inner[:, :, -1].astype(jnp.bfloat16)
    blocks = width // tile
    strict = jnp.triu(jnp.ones((blocks, blocks), jnp.bfloat16), 1)
    before = jnp.einsum("rb,bc->rc", totals, strict, preferred_element_type=jnp.float32)
    return (inner + before[:, :, None]).reshape(rows, width).astype(jnp.int32) - 1


def mixing(source_row, group_index, group_count):
    feat_count = source_row.shape[0] // group_count
    per_peer = feat_count // group_count
    slots = -(-per_peer // LANES) * LANES
    targets = source_row.reshape(group_count, feat_count)
    groups = targets // feat_count
    place = jnp.arange(slots, dtype=jnp.int32)

    mine = groups == group_index
    rank = jnp.where(mine, running_rank(mine), -1)
    feature = targets - group_index * feat_count
    hit = rank[:, None, :] == place[None, :, None]
    chosen = jnp.sum(jnp.where(hit, feature[:, None, :] + 1, 0), axis=2) - 1

    own = lax.dynamic_index_in_dim(groups, group_index, 0, keepdims=False)
    sources = jnp.arange(group_count, dtype=jnp.int32)[:, None]
    member = own[None, :] == sources
    landing = jnp.sum(jnp.where(member, running_rank(member) + sources * slots, 0), axis=0)
    return chosen.reshape(-1), landing, slots


def dot(left, right, left_dim=1, right_dim=0):
    return lax.dot_general(
        left, right, (((left_dim,), (right_dim,)), ((), ())), preferred_element_type=jnp.float32
    )


def relay_kernel(
    sections, groups, slots,
    inputs, last_grads, first, first_turned, second_turned, chosen, landing,
    grads_out, befores_out, cotangents_out, came_out, sent_out, slopes_out,
    leaving, back_mix, cotangents, arrived, slopes, grads, befores, sending,
    in_sem, slope_sem, grad_sem, before_sem, sent_sem, keep_sem,
    send_sem, recv_sem, relay_send, relay_recv, swap_send, swap_recv, swap_own,
):
    section = lax.axis_index("pipe")
    group = lax.axis_index("tensor")
    last = sections - 1
    chunks, rows, feats = inputs.shape
    size = first.shape[1]
    depth = arrived.shape[0]
    tile = 512 if feats % 512 == 0 else 256
    parts = 3 if feats // tile % 3 == 0 else 1
    part = feats // parts
    late = section >= sections - 2

    def peer(offset):
        return lax.rem(group + offset, groups)

    def source(offset):
        return lax.rem(group + (groups - offset), groups)

    barrier = pltpu.get_barrier_semaphore()
    for offset in range(1, groups):
        pl.semaphore_signal(barrier, inc=1, device_id={"tensor": peer(offset)}, device_id_type=MESH)

    for beside in (lax.rem(section + 1, sections), lax.rem(section + last, sections)):
        pl.semaphore_signal(barrier, inc=1, device_id={"pipe": beside}, device_id_type=MESH)
    pl.semaphore_wait(barrier, groups + 1)

    def load_last(chunk):
        return pltpu.make_async_copy(
            last_grads.at[chunk], cotangents.at[chunk], relay_recv.at[chunk, 0]
        )

    @pl.when(section == last)
    def _():
        lax.fori_loop(0, chunks, lambda m, _: (load_last(m).start(), 0)[1], 0)

    def load_input(chunk, slot):
        return pltpu.make_async_copy(inputs.at[chunk], grads.at[slot], in_sem.at[slot])

    step = 256

    def build_leaving(index, _):
        at = pl.ds(pl.multiple_of(index * LANES, LANES), LANES)
        column = chosen[at, :]
        for left in range(0, feats, step):
            lane = lax.broadcasted_iota(jnp.int32, (LANES, step), 1) + left
            leaving[at, left : left + step] = jnp.where(column == lane, 1.0, 0.0).astype(jnp.bfloat16)
        return 0

    lax.fori_loop(0, groups * slots // LANES, build_leaving, 0)

    def build_back(block, _):
        at = pl.ds(pl.multiple_of(block * size, size), size)
        column = landing[at, :]
        turned = second_turned[block]
        for peer_index in range(groups):
            for left in range(0, slots, LANES):
                lane = lax.broadcasted_iota(jnp.int32, (size, LANES), 1) + (peer_index * slots + left)
                spread = jnp.where(column == lane, 1.0, 0.0).astype(jnp.bfloat16)
                back_mix[peer_index, at, left : left + LANES] = dot(turned, spread).astype(jnp.bfloat16)
        return 0

    lax.fori_loop(0, feats // size, build_back, 0)

    def store_slope(chunk, slot):
        return pltpu.make_async_copy(befores.at[slot], slopes_out.at[chunk], before_sem.at[slot])

    def store_sent(chunk, slot):
        return pltpu.make_async_copy(sending.at[slot], sent_out.at[:, chunk], sent_sem.at[slot])

    def forward(with_slope, with_value, chunk, _):
        slot = lax.rem(chunk, 2)
        load_input(chunk, slot).wait()

        @pl.when(chunk + 1 < chunks)
        def _():
            load_input(chunk + 1, 1 - slot).start()

        @pl.when(chunk >= 2)
        def _():
            done(with_slope, with_value, chunk - 2, slot)

        def one_block(block, _):
            at = pl.ds(pl.multiple_of(block * size, size), size)
            value, slope = gelu_both(dot(grads[slot, :, at], first[block]))
            if with_value:
                slopes[0, :, at] = value.astype(jnp.bfloat16)
            if with_slope:
                befores[slot, :, at] = slope.astype(jnp.bfloat16)
            return 0

        lax.fori_loop(0, feats // size, one_block, 0, unroll=2)
        if with_value:
            for target in range(groups):
                sending[slot, target] = dot(
                    slopes[0], leaving[target * slots : (target + 1) * slots, :], 1, 1
                ).astype(jnp.bfloat16)
            store_sent(chunk, slot).start()
        if with_slope:
            store_slope(chunk, slot).start()
        return 0

    def done(with_slope, with_value, chunk, slot):
        if with_slope:
            store_slope(chunk, slot).wait()
        if with_value:
            store_sent(chunk, slot).wait()

    def recompute(with_slope, with_value):
        load_input(0, 0).start()
        lax.fori_loop(0, chunks, functools.partial(forward, with_slope, with_value), 0)
        for chunk in range(chunks - 2, chunks):
            done(with_slope, with_value, chunk, chunk % 2)

    @pl.when(late)
    def _():
        recompute(True, False)

    @pl.when(section < sections - 2)
    def _():
        recompute(True, True)

    def swap(offset):
        return pltpu.make_async_remote_copy(
            src_ref=sent_out.at[peer(offset)],
            dst_ref=came_out.at[group],
            send_sem=swap_send.at[offset],
            recv_sem=swap_recv.at[offset],
            device_id={"tensor": peer(offset)},
            device_id_type=MESH,
        )

    own_swap = pltpu.make_async_copy(sent_out.at[group], came_out.at[group], swap_own)

    def start_swap():
        for offset in range(1, groups):
            swap(offset).start()
        own_swap.start()

    @pl.when(section * 2 < sections)
    def _():
        start_swap()

    def mix_copy(chunk, slot, offset):
        target = peer(offset)
        return pltpu.make_async_remote_copy(
            src_ref=sending.at[slot, target],
            dst_ref=arrived.at[lax.rem(chunk, depth), group],
            send_sem=send_sem.at[slot, offset],
            recv_sem=recv_sem.at[chunk, offset],
            device_id={"tensor": target},
            device_id_type=MESH,
        )

    def mix_wait(chunk, slot, offset):
        origin = source(offset)
        pltpu.make_async_remote_copy(
            src_ref=sending.at[slot, origin],
            dst_ref=arrived.at[lax.rem(chunk, depth), origin],
            send_sem=send_sem.at[slot, offset],
            recv_sem=recv_sem.at[chunk, offset],
            device_id={"tensor": origin},
            device_id_type=MESH,
        ).wait_recv()

    def relay_copy(chunk, slot, target, piece):
        at = pl.ds(piece * part, part)
        return pltpu.make_async_remote_copy(
            src_ref=grads.at[slot, :, at],
            dst_ref=cotangents.at[chunk, :, at],
            send_sem=relay_send.at[slot, piece],
            recv_sem=relay_recv.at[chunk, piece],
            device_id={"pipe": target},
            device_id_type=MESH,
        )

    def load_slope(chunk, slot):
        return pltpu.make_async_copy(slopes_out.at[chunk], slopes.at[slot], slope_sem.at[slot])

    def store_cotangent(chunk):
        return pltpu.make_async_copy(
            cotangents.at[chunk], cotangents_out.at[chunk], keep_sem.at[chunk]
        )

    def store_grad(chunk, slot):
        return pltpu.make_async_copy(grads.at[slot], grads_out.at[chunk], grad_sem.at[slot])

    def store_before(chunk, slot):
        return pltpu.make_async_copy(befores.at[slot], befores_out.at[chunk], before_sem.at[slot])

    def first_half(chunk, slot):
        @pl.when(section == last)
        def _():
            load_last(chunk).wait()

        @pl.when(section < last)
        def _():
            for piece in range(parts):
                relay_copy(chunk, slot, section + 1, piece).wait_recv()

        load_slope(chunk, slot).start()
        store_cotangent(chunk).start()
        for offset in range(1, groups):
            target = peer(offset)
            sending[slot, target] = dot(cotangents[chunk], back_mix[target]).astype(jnp.bfloat16)
            mix_copy(chunk, slot, offset).start()
        arrived[lax.rem(chunk, depth), group] = dot(cotangents[chunk], back_mix[group]).astype(
            jnp.bfloat16
        )

    def leave(chunk, slot):
        store_grad(chunk, slot).wait()
        store_before(chunk, slot).wait()

        @pl.when(section > 0)
        def _():
            for piece in range(parts):
                relay_copy(chunk, slot, section - 1, piece).wait_send()

    def second_half(chunk, slot):
        for offset in range(1, groups):
            mix_wait(chunk, slot, offset)
        load_slope(chunk, slot).wait()

        @pl.when(chunk >= 2)
        def _():
            leave(chunk - 2, slot)

        held = lax.rem(chunk, depth)

        def one_tile(index, _):
            start = pl.multiple_of(index * tile, tile)
            at = pl.ds(start, tile)
            total = dot(arrived[held, 0], leaving[0:slots, at])
            for origin in range(1, groups):
                total += dot(
                    arrived[held, origin], leaving[origin * slots : (origin + 1) * slots, at]
                )
            before = (total * slopes[slot, :, at].astype(jnp.float32)).astype(jnp.bfloat16)
            befores[slot, :, at] = before
            for piece in range(tile // size):
                here = pl.ds(pl.multiple_of(start + piece * size, size), size)
                back = dot(
                    before[:, piece * size : (piece + 1) * size],
                    first_turned[index * (tile // size) + piece],
                )
                grads[slot, :, here] = (
                    cotangents[chunk, :, here].astype(jnp.float32) + back
                ).astype(jnp.bfloat16)
            return 0

        each = feats // tile // parts
        for piece in range(parts):
            lax.fori_loop(piece * each, (piece + 1) * each, one_tile, 0)

            @pl.when(section > 0)
            def _():
                relay_copy(chunk, slot, section - 1, piece).start()

        store_grad(chunk, slot).start()
        store_before(chunk, slot).start()
        for offset in range(1, groups):
            mix_copy(chunk, slot, offset).wait_send()

    first_half(0, 0)

    def advance(chunk, _):
        slot = lax.rem(chunk, 2)

        @pl.when(chunk + 1 < chunks)
        def _():
            first_half(chunk + 1, 1 - slot)

        second_half(chunk, slot)
        return 0

    lax.fori_loop(0, chunks, advance, 0)

    for chunk in range(chunks - 2, chunks):
        leave(chunk, chunk % 2)

    @pl.when(late)
    def _():
        recompute(False, True)

    @pl.when(section * 2 >= sections)
    def _():
        start_swap()

    lax.fori_loop(0, chunks, lambda m, _: (store_cotangent(m).wait(), 0)[1], 0)
    for offset in range(1, groups):
        swap(offset).wait()
    own_swap.wait()


def weight_kernel(came, landing, kept, cotangents, inputs, befores, first_out, second_out):
    groups, tokens, slots = came.shape
    count, size, _ = first_out.shape
    where = landing[...]
    mixed = jnp.zeros((tokens, where.shape[1]), jnp.float32)
    for origin in range(groups):
        slot = lax.broadcasted_iota(jnp.int32, (slots, where.shape[1]), 0) + origin * slots
        spread = jnp.where(slot == where, 1.0, 0.0).astype(jnp.bfloat16)
        mixed += dot(came[origin], spread)
    mixed = mixed.astype(jnp.bfloat16)
    for piece in range(count):
        at = slice(piece * size, (piece + 1) * size)
        second_out[piece] = dot(mixed[:, at], cotangents[:, at], 0, 0) * kept[0, 0]
        first_out[piece] = dot(inputs[:, at], befores[:, at], 0, 0)


def on_device(section_inputs, out_grad, w_first, w_second, drop_flags, perm):
    sections = lax.axis_size("pipe")
    groups = lax.axis_size("tensor")
    _, micro_count, token_count, feats = section_inputs.shape
    tokens = micro_count * token_count
    first = w_first[0, 0]
    blocks, size, _ = first.shape
    kept = drop_flags[0, 0]
    chosen, landing, slots = mixing(perm[0, 0], lax.axis_index("tensor"), groups)
    rows = ROWS
    chunks = tokens // rows
    depth = min(4, chunks)
    chunked = (chunks, rows, feats)

    def made(*shape):
        return jax.ShapeDtypeStruct(shape, jnp.bfloat16)

    def room(*shape):
        return pltpu.VMEM(shape, jnp.bfloat16)

    sem = pltpu.SemaphoreType.DMA
    anywhere = pl.BlockSpec(memory_space=pl.ANY)
    vmem = pl.BlockSpec(memory_space=pltpu.VMEM)
    swapped = (groups, chunks, rows, slots)
    grads, befores, cotangents, came, _, _ = pl.pallas_call(
        functools.partial(relay_kernel, sections, groups, slots),
        out_shape=[made(*chunked)] * 3 + [made(*swapped)] * 2 + [made(*chunked)],
        in_specs=[anywhere] * 2 + [vmem] * 5,
        out_specs=[anywhere] * 6,
        scratch_shapes=[
            room(groups * slots, feats),
            room(groups, feats, slots),
            room(*chunked),
            room(depth, groups, rows, slots),
            room(2, rows, feats),
            room(2, rows, feats),
            room(2, rows, feats),
            room(2, groups, rows, slots),
            sem((2,)), sem((2,)), sem((2,)), sem((2,)), sem((2,)), sem((chunks,)),
            sem((2, groups)), sem((chunks, groups)), sem((2, 3)), sem((chunks, 3)),
            sem((groups,)), sem((groups,)), sem(()),
        ],
        compiler_params=pltpu.CompilerParams(
            collective_id=0, has_side_effects=True, vmem_limit_bytes=62 * 2**20
        ),
    )(
        section_inputs.reshape(chunked),
        out_grad.reshape(chunked),
        first,
        jnp.swapaxes(first, 1, 2),
        jnp.swapaxes(w_second[0, 0], 1, 2) * kept.astype(jnp.bfloat16),
        chosen[:, None],
        landing[:, None],
    )

    wide = 256
    tall = pl.BlockSpec((tokens, wide), lambda i: (0, i))
    out = pl.BlockSpec((wide // size, size, size), lambda i: (i, 0, 0))
    weights = jax.ShapeDtypeStruct((blocks, size, size), jnp.float32)
    first_grad, second_grad = pl.pallas_call(
        weight_kernel,
        grid=(feats // wide,),
        out_shape=[weights] * 2,
        in_specs=[
            pl.BlockSpec((groups, tokens, slots), lambda i: (0, 0, 0)),
            pl.BlockSpec((1, wide), lambda i: (0, i)),
            pl.BlockSpec(memory_space=pltpu.SMEM),
            tall, tall, tall,
        ],
        out_specs=[out] * 2,
        compiler_params=pltpu.CompilerParams(vmem_limit_bytes=56 * 2**20),
    )(
        came.reshape(groups, tokens, slots),
        landing[None, :],
        kept.astype(jnp.float32).reshape(1, 1),
        cotangents.reshape(tokens, feats),
        section_inputs.reshape(tokens, feats),
        befores.reshape(tokens, feats),
    )
    return grads.reshape(section_inputs.shape), first_grad[None, None], second_grad[None, None]


def solution(mesh):
    placed = (
        P("pipe", None, None, "tensor"),
        P(None, None, "tensor"),
        P("pipe", None, "tensor", None, None),
        P("pipe", None, "tensor", None, None),
        P("pipe", None),
        P("pipe", None, None),
    )
    return jax.shard_map(
        on_device,
        mesh=mesh,
        in_specs=placed,
        out_specs=(
            P("pipe", None, None, "tensor"),
            P("pipe", None, "tensor", None, None),
            P("pipe", None, "tensor", None, None),
        ),
        check_vma=False,
    )
```

```python
import functools

import jax
import jax.numpy as jnp
from jax import lax
from jax.experimental import pallas as pl
from jax.experimental.pallas import tpu as pltpu
from jax.sharding import PartitionSpec as P

gelu_scale = 0.7978845608028654
gelu_cubic = 0.044715
LANES = 128
ROWS = 128
MESH = pl.DeviceIdType.MESH


def gelu_both(values):
    square = values * values
    tangent = jnp.tanh(gelu_scale * (values + gelu_cubic * square * values))
    value = 0.5 * values * (1.0 + tangent)
    slope = 0.5 * (1.0 + tangent) + 0.5 * values * (1.0 - tangent * tangent) * gelu_scale * (
        1.0 + 3.0 * gelu_cubic * square
    )
    return value, slope


def running_rank(member):
    rows, width = member.shape
    tile = LANES
    pieces = member.reshape(rows, width // tile, tile).astype(jnp.bfloat16)
    upper = jnp.triu(jnp.ones((tile, tile), jnp.bfloat16))
    inner = jnp.einsum("rbi,ij->rbj", pieces, upper, preferred_element_type=jnp.float32)
    totals = inner[:, :, -1].astype(jnp.bfloat16)
    blocks = width // tile
    strict = jnp.triu(jnp.ones((blocks, blocks), jnp.bfloat16), 1)
    before = jnp.einsum("rb,bc->rc", totals, strict, preferred_element_type=jnp.float32)
    return (inner + before[:, :, None]).reshape(rows, width).astype(jnp.int32) - 1


def mixing(source_row, group_index, group_count):
    feat_count = source_row.shape[0] // group_count
    per_peer = feat_count // group_count
    slots = -(-per_peer // LANES) * LANES
    targets = source_row.reshape(group_count, feat_count)
    groups = targets // feat_count
    place = jnp.arange(slots, dtype=jnp.int32)

    mine = groups == group_index
    rank = jnp.where(mine, running_rank(mine), -1)
    feature = targets - group_index * feat_count
    hit = rank[:, None, :] == place[None, :, None]
    chosen = jnp.sum(jnp.where(hit, feature[:, None, :] + 1, 0), axis=2) - 1

    own = lax.dynamic_index_in_dim(groups, group_index, 0, keepdims=False)
    sources = jnp.arange(group_count, dtype=jnp.int32)[:, None]
    member = own[None, :] == sources
    landing = jnp.sum(jnp.where(member, running_rank(member) + sources * slots, 0), axis=0)
    return chosen.reshape(-1), landing, slots


def dot(left, right, left_dim=1, right_dim=0):
    return lax.dot_general(
        left, right, (((left_dim,), (right_dim,)), ((), ())), preferred_element_type=jnp.float32
    )


def relay_kernel(
    sections, groups, slots,
    inputs, last_grads, first, first_turned, second_turned, chosen, landing,
    grads_out, befores_out, cotangents_out, came_out, sent_out, slopes_out,
    leaving, back_mix, cotangents, arrived, slopes, grads, befores, sending,
    in_sem, slope_sem, grad_sem, before_sem, sent_sem, keep_sem,
    send_sem, recv_sem, relay_send, relay_recv, swap_send, swap_recv, swap_own,
):
    section = lax.axis_index("pipe")
    group = lax.axis_index("tensor")
    last = sections - 1
    chunks, rows, feats = inputs.shape
    size = first.shape[1]
    depth = arrived.shape[0]

    def columns(origin):
        return pl.ds(pl.multiple_of(origin * slots, LANES), slots)

    tile = 512 if feats % 512 == 0 else 256
    parts = 3 if feats // tile % 3 == 0 else 1
    part = feats // parts
    late = section >= sections - 2

    def peer(offset):
        return lax.rem(group + offset, groups)

    def source(offset):
        return lax.rem(group + (groups - offset), groups)

    barrier = pltpu.get_barrier_semaphore()
    for offset in range(1, groups):
        pl.semaphore_signal(barrier, inc=1, device_id={"tensor": peer(offset)}, device_id_type=MESH)

    for beside in (lax.rem(section + 1, sections), lax.rem(section + last, sections)):
        pl.semaphore_signal(barrier, inc=1, device_id={"pipe": beside}, device_id_type=MESH)
    pl.semaphore_wait(barrier, groups + 1)

    def load_last(chunk):
        return pltpu.make_async_copy(
            last_grads.at[chunk], cotangents.at[chunk], relay_recv.at[chunk, 0]
        )

    @pl.when(section == last)
    def _():
        lax.fori_loop(0, chunks, lambda m, _: (load_last(m).start(), 0)[1], 0)

    def load_input(chunk, slot):
        return pltpu.make_async_copy(inputs.at[chunk], grads.at[slot], in_sem.at[slot])

    step = 256

    def build_leaving(index, _):
        at = pl.ds(pl.multiple_of(index * LANES, LANES), LANES)
        column = chosen[at, :]
        for left in range(0, feats, step):
            lane = lax.broadcasted_iota(jnp.int32, (LANES, step), 1) + left
            leaving[at, left : left + step] = jnp.where(column == lane, 1.0, 0.0).astype(jnp.bfloat16)
        return 0

    lax.fori_loop(0, groups * slots // LANES, build_leaving, 0)

    def build_back(block, _):
        at = pl.ds(pl.multiple_of(block * size, size), size)
        column = landing[at, :]
        turned = second_turned[block]
        for peer_index in range(groups):
            for left in range(0, slots, LANES):
                lane = lax.broadcasted_iota(jnp.int32, (size, LANES), 1) + (peer_index * slots + left)
                spread = jnp.where(column == lane, 1.0, 0.0).astype(jnp.bfloat16)
                back_mix[peer_index, at, left : left + LANES] = dot(turned, spread).astype(jnp.bfloat16)
        return 0

    lax.fori_loop(0, feats // size, build_back, 0)

    def store_slope(chunk, slot):
        return pltpu.make_async_copy(befores.at[slot], slopes_out.at[chunk], before_sem.at[slot])

    def store_sent(chunk, slot):
        return pltpu.make_async_copy(sending.at[slot], sent_out.at[:, chunk], sent_sem.at[slot])

    def forward(with_slope, with_value, chunk, _):
        slot = lax.rem(chunk, 2)
        load_input(chunk, slot).wait()

        @pl.when(chunk + 1 < chunks)
        def _():
            load_input(chunk + 1, 1 - slot).start()

        @pl.when(chunk >= 2)
        def _():
            done(with_slope, with_value, chunk - 2, slot)

        def one_block(block, _):
            at = pl.ds(pl.multiple_of(block * size, size), size)
            value, slope = gelu_both(dot(grads[slot, :, at], first[block]))
            if with_value:
                slopes[0, :, at] = value.astype(jnp.bfloat16)
            if with_slope:
                befores[slot, :, at] = slope.astype(jnp.bfloat16)
            return 0

        lax.fori_loop(0, feats // size, one_block, 0, unroll=2)
        if with_value:
            for target in range(groups):
                sending[slot, target] = dot(
                    slopes[0], leaving[target * slots : (target + 1) * slots, :], 1, 1
                ).astype(jnp.bfloat16)
            store_sent(chunk, slot).start()
        if with_slope:
            store_slope(chunk, slot).start()
        return 0

    def done(with_slope, with_value, chunk, slot):
        if with_slope:
            store_slope(chunk, slot).wait()
        if with_value:
            store_sent(chunk, slot).wait()

    def recompute(with_slope, with_value):
        load_input(0, 0).start()
        lax.fori_loop(0, chunks, functools.partial(forward, with_slope, with_value), 0)
        for chunk in range(chunks - 2, chunks):
            done(with_slope, with_value, chunk, chunk % 2)

    @pl.when(late)
    def _():
        recompute(True, False)

    @pl.when(section < sections - 2)
    def _():
        recompute(True, True)

    def swap(offset):
        return pltpu.make_async_remote_copy(
            src_ref=sent_out.at[peer(offset)],
            dst_ref=came_out.at[:, :, columns(group)],
            send_sem=swap_send.at[offset],
            recv_sem=swap_recv.at[offset],
            device_id={"tensor": peer(offset)},
            device_id_type=MESH,
        )

    own_swap = pltpu.make_async_copy(
        sent_out.at[group], came_out.at[:, :, columns(group)], swap_own
    )

    def start_swap():
        for offset in range(1, groups):
            swap(offset).start()
        own_swap.start()

    @pl.when(section * 2 < sections)
    def _():
        start_swap()

    def mix_copy(chunk, slot, offset):
        target = peer(offset)
        return pltpu.make_async_remote_copy(
            src_ref=sending.at[slot, target],
            dst_ref=arrived.at[lax.rem(chunk, depth), :, columns(group)],
            send_sem=send_sem.at[slot, offset],
            recv_sem=recv_sem.at[chunk, offset],
            device_id={"tensor": target},
            device_id_type=MESH,
        )

    def mix_wait(chunk, slot, offset):
        origin = source(offset)
        pltpu.make_async_remote_copy(
            src_ref=sending.at[slot, origin],
            dst_ref=arrived.at[lax.rem(chunk, depth), :, columns(origin)],
            send_sem=send_sem.at[slot, offset],
            recv_sem=recv_sem.at[chunk, offset],
            device_id={"tensor": origin},
            device_id_type=MESH,
        ).wait_recv()

    def relay_copy(chunk, slot, target, piece):
        at = pl.ds(piece * part, part)
        return pltpu.make_async_remote_copy(
            src_ref=grads.at[slot, :, at],
            dst_ref=cotangents.at[chunk, :, at],
            send_sem=relay_send.at[slot, piece],
            recv_sem=relay_recv.at[chunk, piece],
            device_id={"pipe": target},
            device_id_type=MESH,
        )

    def load_slope(chunk, slot):
        return pltpu.make_async_copy(slopes_out.at[chunk], slopes.at[slot], slope_sem.at[slot])

    def store_cotangent(chunk):
        return pltpu.make_async_copy(
            cotangents.at[chunk], cotangents_out.at[chunk], keep_sem.at[chunk]
        )

    def store_grad(chunk, slot):
        return pltpu.make_async_copy(grads.at[slot], grads_out.at[chunk], grad_sem.at[slot])

    def store_before(chunk, slot):
        return pltpu.make_async_copy(befores.at[slot], befores_out.at[chunk], before_sem.at[slot])

    def first_half(chunk, slot):
        @pl.when(section == last)
        def _():
            load_last(chunk).wait()

        @pl.when(section < last)
        def _():
            for piece in range(parts):
                relay_copy(chunk, slot, section + 1, piece).wait_recv()

        load_slope(chunk, slot).start()
        store_cotangent(chunk).start()
        for offset in range(1, groups):
            target = peer(offset)
            sending[slot, target] = dot(cotangents[chunk], back_mix[target]).astype(jnp.bfloat16)
            mix_copy(chunk, slot, offset).start()
        arrived[lax.rem(chunk, depth), :, columns(group)] = dot(
            cotangents[chunk], back_mix[group]
        ).astype(jnp.bfloat16)

    def leave(chunk, slot):
        store_grad(chunk, slot).wait()
        store_before(chunk, slot).wait()

        @pl.when(section > 0)
        def _():
            for piece in range(parts):
                relay_copy(chunk, slot, section - 1, piece).wait_send()

    def second_half(chunk, slot):
        for offset in range(1, groups):
            mix_wait(chunk, slot, offset)
        load_slope(chunk, slot).wait()

        @pl.when(chunk >= 2)
        def _():
            leave(chunk - 2, slot)

        held = lax.rem(chunk, depth)

        def one_tile(index, _):
            start = pl.multiple_of(index * tile, tile)
            at = pl.ds(start, tile)
            total = dot(arrived[held], leaving[:, at])
            before = (total * slopes[slot, :, at].astype(jnp.float32)).astype(jnp.bfloat16)
            befores[slot, :, at] = before
            for piece in range(tile // size):
                here = pl.ds(pl.multiple_of(start + piece * size, size), size)
                back = dot(
                    before[:, piece * size : (piece + 1) * size],
                    first_turned[index * (tile // size) + piece],
                )
                grads[slot, :, here] = (
                    cotangents[chunk, :, here].astype(jnp.float32) + back
                ).astype(jnp.bfloat16)
            return 0

        each = feats // tile // parts
        for piece in range(parts):
            lax.fori_loop(piece * each, (piece + 1) * each, one_tile, 0)

            @pl.when(section > 0)
            def _():
                relay_copy(chunk, slot, section - 1, piece).start()

        store_grad(chunk, slot).start()
        store_before(chunk, slot).start()
        for offset in range(1, groups):
            mix_copy(chunk, slot, offset).wait_send()

    first_half(0, 0)

    def advance(chunk, _):
        slot = lax.rem(chunk, 2)

        @pl.when(chunk + 1 < chunks)
        def _():
            first_half(chunk + 1, 1 - slot)

        second_half(chunk, slot)
        return 0

    lax.fori_loop(0, chunks, advance, 0)

    for chunk in range(chunks - 2, chunks):
        leave(chunk, chunk % 2)

    @pl.when(late)
    def _():
        recompute(False, True)

    @pl.when(section * 2 >= sections)
    def _():
        start_swap()

    lax.fori_loop(0, chunks, lambda m, _: (store_cotangent(m).wait(), 0)[1], 0)
    for offset in range(1, groups):
        swap(offset).wait()
    own_swap.wait()


def weight_kernel(came, landing, kept, cotangents, inputs, befores, first_out, second_out):
    count, size, _ = first_out.shape
    where = landing[...]
    slot = lax.broadcasted_iota(jnp.int32, (came.shape[1], where.shape[1]), 0)
    spread = jnp.where(slot == where, 1.0, 0.0).astype(jnp.bfloat16)
    mixed = dot(came[...], spread).astype(jnp.bfloat16)
    second = dot(mixed, cotangents[...], 0, 0) * kept[0, 0]
    first = dot(inputs[...], befores[...], 0, 0)
    for piece in range(count):
        at = slice(piece * size, (piece + 1) * size)
        second_out[piece] = second[at, at]
        first_out[piece] = first[at, at]


def on_device(section_inputs, out_grad, w_first, w_second, drop_flags, perm):
    sections = lax.axis_size("pipe")
    groups = lax.axis_size("tensor")
    _, micro_count, token_count, feats = section_inputs.shape
    tokens = micro_count * token_count
    first = w_first[0, 0]
    blocks, size, _ = first.shape
    kept = drop_flags[0, 0]
    chosen, landing, slots = mixing(perm[0, 0], lax.axis_index("tensor"), groups)
    rows = ROWS
    chunks = tokens // rows
    depth = min(4, chunks)
    chunked = (chunks, rows, feats)

    def made(*shape):
        return jax.ShapeDtypeStruct(shape, jnp.bfloat16)

    def room(*shape):
        return pltpu.VMEM(shape, jnp.bfloat16)

    sem = pltpu.SemaphoreType.DMA
    anywhere = pl.BlockSpec(memory_space=pl.ANY)
    vmem = pl.BlockSpec(memory_space=pltpu.VMEM)
    swapped = (groups, chunks, rows, slots)
    grads, befores, cotangents, came, _, _ = pl.pallas_call(
        functools.partial(relay_kernel, sections, groups, slots),
        out_shape=[made(*chunked)] * 3
        + [made(chunks, rows, groups * slots), made(*swapped), made(*chunked)],
        in_specs=[anywhere] * 2 + [vmem] * 5,
        out_specs=[anywhere] * 6,
        scratch_shapes=[
            room(groups * slots, feats),
            room(groups, feats, slots),
            room(*chunked),
            room(depth, rows, groups * slots),
            room(2, rows, feats),
            room(2, rows, feats),
            room(2, rows, feats),
            room(2, groups, rows, slots),
            sem((2,)), sem((2,)), sem((2,)), sem((2,)), sem((2,)), sem((chunks,)),
            sem((2, groups)), sem((chunks, groups)), sem((2, 3)), sem((chunks, 3)),
            sem((groups,)), sem((groups,)), sem(()),
        ],
        compiler_params=pltpu.CompilerParams(
            collective_id=0, has_side_effects=True, vmem_limit_bytes=62 * 2**20
        ),
    )(
        section_inputs.reshape(chunked),
        out_grad.reshape(chunked),
        first,
        jnp.swapaxes(first, 1, 2),
        jnp.swapaxes(w_second[0, 0], 1, 2) * kept.astype(jnp.bfloat16),
        chosen[:, None],
        landing[:, None],
    )

    wide = 256
    tall = pl.BlockSpec((tokens, wide), lambda i: (0, i))
    out = pl.BlockSpec((wide // size, size, size), lambda i: (i, 0, 0))
    weights = jax.ShapeDtypeStruct((blocks, size, size), jnp.float32)
    first_grad, second_grad = pl.pallas_call(
        weight_kernel,
        grid=(feats // wide,),
        out_shape=[weights] * 2,
        in_specs=[
            pl.BlockSpec((tokens, groups * slots), lambda i: (0, 0)),
            pl.BlockSpec((1, wide), lambda i: (0, i)),
            pl.BlockSpec(memory_space=pltpu.SMEM),
            tall, tall, tall,
        ],
        out_specs=[out] * 2,
        compiler_params=pltpu.CompilerParams(vmem_limit_bytes=56 * 2**20),
    )(
        came.reshape(tokens, groups * slots),
        landing[None, :],
        kept.astype(jnp.float32).reshape(1, 1),
        cotangents.reshape(tokens, feats),
        section_inputs.reshape(tokens, feats),
        befores.reshape(tokens, feats),
    )
    return grads.reshape(section_inputs.shape), first_grad[None, None], second_grad[None, None]


def solution(mesh):
    placed = (
        P("pipe", None, None, "tensor"),
        P(None, None, "tensor"),
        P("pipe", None, "tensor", None, None),
        P("pipe", None, "tensor", None, None),
        P("pipe", None),
        P("pipe", None, None),
    )
    return jax.shard_map(
        on_device,
        mesh=mesh,
        in_specs=placed,
        out_specs=(
            P("pipe", None, None, "tensor"),
            P("pipe", None, "tensor", None, None),
            P("pipe", None, "tensor", None, None),
        ),
        check_vma=False,
    )
```
